128 devices in a mesh: dom: 8 (over y, core), row: 16 (over x, z).
Axes of the slice: x: 4, y: 4, z: 4, core: 2. Of those that a mesh axis runs over, the one named last changes fastest.
Arguments:
- diag_blocks: float32 [2048, 384, 384], P(('dom', 'row')), may hold values from -0.2 to 1.5
- outgoing: float32 [16, 32, 384, 384], P('dom', 'row'), may hold values from -3 to 3
- arrive_elem: int32 [16, 32], P('dom', 'row'), may hold values from 0 to 15
- owner_row: int32 [2048], P(('dom', 'row')), may hold values from 0 to 16, as said below
Outputs:
- inverse_blocks: float32 [2048, 384, 384], P(('dom', 'row'))
- scaled: float32 [16, 32, 384, 384], P('dom', 'row')
The draws below stay inside these ranges and needn't reach their ends.
Inputs may be any that keep to these rules, and one draw needn't show every extreme that they name: `owner_row`: within each index of dom, every owner receives exactly 4 stiff rows, no device has two stiff rows with the same owner, and some device of each index of dom has all 16 rows stiff.
All inputs are finite; a program needn't handle non-finite values.
Results may differ from the reference program's by a relative error of at most 0.0001.
Values sent between devices are 32-bit elements; how exact they have to be, the bound alone decides.
No kernel may reach another device: no remote copies, remote signals or barrier semaphores. Data moves between devices by JAX's collectives and lax.ppermute only.
A program may use at most 256 MiB of HBM per device.

```python
import math
import jax
import jax.numpy as jnp
from jax import lax

L = 384
E_DEV = 16
FACE = 2
NS_ITERS = 6
ELEMS = 2048
N_DOM = 8
N_ROW = 16


def draw_diag_blocks(key, part):
    first_key, second_key = jax.random.split(jax.random.fold_in(key, 5))
    diag_vals = jax.random.uniform(first_key, (ELEMS, L), jnp.float32, 1.0, 1.25)
    spread = 0.45 / math.sqrt(L)
    clip_edge = min(6.0 * spread, 0.15)
    noise = jnp.clip(jax.random.normal(second_key, (ELEMS, L, L), jnp.float32) * spread, -clip_edge, clip_edge)
    return noise + diag_vals[:, :, None] * jnp.eye(L, dtype=jnp.float32)[None, :, :]


def owner_group(group_key):
    quota = E_DEV // 4
    quads = N_ROW // 4
    pair_key, take_key, owner_key, rank_key = jax.random.split(group_key, 4)
    sources = jax.random.permutation(pair_key, N_ROW).astype(jnp.int32)
    takes = jax.random.randint(take_key, (quads, 3), 0, quota + 1).astype(jnp.int32)
    takes = takes.at[0].set(quota)
    leader = quota + jnp.sum(takes, axis=1)
    members = quota - takes
    quad_counts = jnp.concatenate([leader[:, None], members], axis=1).reshape(-1)
    counts = jnp.zeros((N_ROW,), jnp.int32).at[sources].set(quad_counts)
    offsets = jnp.cumsum(counts) - counts
    owner_perm = jax.random.permutation(owner_key, N_ROW).astype(jnp.int32)
    device_keys = jax.random.split(rank_key, N_ROW)

    def ranking(device_key):
        return jnp.argsort(jax.random.permutation(device_key, E_DEV).astype(jnp.int32)).astype(jnp.int32)
    ranks = jax.vmap(ranking)(device_keys)
    position = offsets[:, None] + ranks
    owners = owner_perm[position % N_ROW]
    return jnp.where(ranks < counts[:, None], owners, N_ROW).astype(jnp.int32)


def draw_owner_row(key, part):
    group_keys = jax.random.split(jax.random.fold_in(key, 11), N_DOM)
    return jax.vmap(owner_group)(group_keys).reshape(-1).astype(jnp.int32)


def place_ends(values, stream_key, low, top_value):
    shape = values.shape
    place = [jax.random.randint(jax.random.fold_in(stream_key, axis), (), 0, shape[axis]) for axis in range(len(shape))]
    values = values.at[tuple(place)].set(low)
    longest = shape.index(max(shape))
    place[longest] = (place[longest] + 1) % shape[longest]
    return values.at[tuple(place)].set(top_value)


def levels(stream_key, extent, cuts, smallest, high):
    def one(dim, shards_of):
        heights = jax.random.uniform(jax.random.fold_in(jax.random.fold_in(stream_key, 6), dim), (shards_of,), jnp.float32, smallest / len(cuts), high / len(cuts))
        return jnp.repeat(jnp.exp(heights), extent[dim] // shards_of).reshape((-1,) + (1,) * (len(extent) - dim - 1))

    factor_of = one(*cuts[0])
    for cut in cuts[1:]:
        factor_of = factor_of * one(*cut)
    return factor_of


def normal_values(key, shape, width, reach, cuts=(), kind=jnp.bfloat16):
    drawn = width * jax.random.normal(key, shape, jnp.float32)
    if cuts:
        drawn = drawn * levels(key, shape, cuts, -0.22, 0.18)
    return jnp.clip(drawn, -reach, reach).astype(kind)


def setup_inputs(seed: int = 0) -> dict:
    keys = jax.random.split(jax.random.key(seed), 5)
    diag_blocks = draw_diag_blocks(jax.random.fold_in(keys[4], 71), 0)
    outgoing = normal_values(keys[1], (2 * N_DOM, N_ROW * FACE, L, L), 0.5, 3.0, ((0, 8), (1, 16)), jnp.float32)
    arrive_elem = place_ends(jax.random.randint(keys[2], (2 * N_DOM, N_ROW * FACE), 0, E_DEV), jax.random.fold_in(keys[2], 1), 0, E_DEV - 1).astype(jnp.int32)
    owner_row = draw_owner_row(jax.random.fold_in(keys[4], 71), 0)
    return dict(diag_blocks=diag_blocks, outgoing=outgoing, arrive_elem=arrive_elem, owner_row=owner_row)


def point_inverse(blocks):
    diag_vals = jnp.diagonal(blocks, axis1=1, axis2=2)
    identity = jnp.eye(blocks.shape[-1], dtype=jnp.float32)
    return identity[None, :, :] / diag_vals[:, None, :]


def newton(blocks):
    identity = jnp.eye(blocks.shape[-1], dtype=jnp.float32)
    current = point_inverse(blocks)
    for repeat in range(NS_ITERS):
        product = jnp.einsum("eij,ejk->eik", blocks, current, precision=lax.Precision.HIGHEST)
        current = jnp.einsum("eij,ejk->eik", current, 2.0 * identity - product, precision=lax.Precision.HIGHEST)
    return current


def scale_pair(pair):
    return jnp.einsum("eij,ejk->eik", pair[0], pair[1], precision=lax.Precision.HIGHEST)


def reference(diag_blocks, outgoing, arrive_elem, owner_row):
    solved = lax.map(newton, diag_blocks.reshape((-1, 8, L, L))).reshape(diag_blocks.shape)
    stiff = owner_row < N_ROW
    inverse_blocks = jnp.where(stiff[:, None, None], solved, point_inverse(diag_blocks))
    tiles = outgoing.reshape((N_DOM, 2, N_ROW * FACE, L, L))
    empty = jnp.zeros((1, N_ROW * FACE, L, L), jnp.float32)
    from_lower = jnp.concatenate([empty, tiles[:-1, 1]], axis=0)
    from_upper = jnp.concatenate([tiles[1:, 0], empty], axis=0)
    incoming = jnp.stack([from_lower, from_upper], axis=1).reshape((-1, 8, L, L))
    local_index = arrive_elem.reshape((N_DOM, 2, N_ROW, FACE)).astype(jnp.int32)
    base = (jnp.arange(N_DOM, dtype=jnp.int32)[:, None, None, None] * N_ROW
            + jnp.arange(N_ROW, dtype=jnp.int32)[None, None, :, None]) * E_DEV
    global_index = (base + local_index).reshape(-1).astype(jnp.int32)
    picked = inverse_blocks[global_index].reshape((-1, 8, L, L))
    scaled = lax.map(scale_pair, (picked, incoming)).reshape(outgoing.shape)
    return inverse_blocks, scaled
```

```python
import functools
import jax
import jax.numpy as jnp
from jax import lax
from jax.experimental import pallas as pl
from jax.experimental.pallas import tpu as pltpu
from jax.sharding import PartitionSpec as P
F8 = jnp.float8_e4m3fn
BF = jnp.bfloat16
F32 = jnp.float32
L = 384
CQ = 2.0**10
CS = (0, 2.0**10, 2.0**12, 2.0**14, 2.0**16)
CLO = 2.0**18
CE = 2.0**14
TOL = 4e-5

def mm(a, b):
    return jnp.dot(a, b, preferred_element_type=F32)

def newton_kernel(G, owners, flag_ref, a_ref, o_ref, rb, rlo, w, acc, qb, q8, eb, e8, f8s, u):
    step = pl.program_id(0)
    rows = lax.broadcasted_iota(jnp.int32, (L, L), 0)
    cols = lax.broadcasted_iota(jnp.int32, (L, L), 1)
    eye = jnp.where(rows == cols, F32(1), F32(0))
    stiff = [flag_ref[step * G + g] < owners for g in range(G)]

    def inv_row(a):
        return 1.0 / jnp.sum(jnp.where(rows == cols, a, 0.0), axis=0, keepdims=True)

    def inv_col(a):
        return 1.0 / jnp.sum(jnp.where(rows == cols, a, 0.0), axis=1, keepdims=True)

    any_stiff = functools.reduce(jnp.logical_or, stiff)

    @pl.when(jnp.logical_not(any_stiff))
    def _():
        for g in range(G):
            o_ref[g] = jnp.where(rows == cols, inv_col(a_ref[g]), 0.0)

    @pl.when(any_stiff)
    def _():
        R = lambda g: eye - a_ref[g] * inv_row(a_ref[g])
        for g in range(G):
            r = R(g)
            b = r.astype(BF)
            rb[g] = b
            rlo[g] = ((r - b.astype(F32)) * CLO).astype(F8)
            w[0, g, :, L:] = (r * CQ).astype(F8)
        for g in range(G):
            s1 = mm(rb[g], rb[g])
            acc[g] = R(g) + s1
            w[0, g, :, :L] = (s1 * CS[1]).astype(F8)
        for k in (1, 2, 3):
            p, n = (k - 1) % 2, k % 2
            for g in range(G):
                d = mm(w[p, g, :, :L], w[p, g])
                t = d[:, L:] * (1.0 / (CS[k] * CQ))
                s = d[:, :L]
                q = acc[g] + t
                w[n, g, :, :L] = (s * (CS[k + 1] / (CS[k] * CS[k]))).astype(F8)
                w[n, g, :, L:] = (q * CQ).astype(F8)
                acc[g] = q + s * (1.0 / (CS[k] * CS[k]))
        for g in range(G):
            t = mm(w[1, g, :, :L], w[1, g, :, L:])
            q = acc[g] + t * (1.0 / (CS[4] * CQ))
            qb[g] = q.astype(BF)
            q8[g] = (q * CQ).astype(F8)
        for g in range(G):
            u[g] = mm(rb[g], qb[g]) + R(g) - qb[g].astype(F32)
        for g in range(G):
            e = u[g] + mm(rlo[g], q8[g]) * (1.0 / (CLO * CQ))
            u[g] = e
            eb[g] = e.astype(BF)
            e8[g] = (e * CE).astype(F8)
        ss = []
        for g in range(G):
            v = mm(qb[g], eb[g])
            f = u[g] + v
            f8s[g] = (f * CE).astype(F8)
            x = inv_col(a_ref[g]) * (eye + qb[g].astype(F32) + f)
            point = jnp.where(rows == cols, inv_col(a_ref[g]), 0.0)
            o_ref[g] = jnp.where(stiff[g], x, point)
            ss.append(jnp.sum(x * x))
        for g in range(G):
            z = inv_col(a_ref[g]) * mm(f8s[g], e8[g])
            zz = jnp.sum(z * z) * (1.0 / (CE * CE))**2
            ok = zz <= (TOL * TOL) * ss[g]

            @pl.when(jnp.logical_and(stiff[g], jnp.logical_not(ok)))
            def _(g=g):
                slow(a_ref, o_ref, u, acc, g, eye, inv_col)

def slow(a_ref, o_ref, u, acc, g, eye, inv_col):
    HI = lax.Precision.HIGHEST
    u[g] = eye * inv_col(a_ref[g])
    def it(i, c):
        acc[g] = 2.0 * eye - jnp.dot(a_ref[g], u[g], precision=HI, preferred_element_type=F32)
        u[g] = jnp.dot(u[g], acc[g], precision=HI, preferred_element_type=F32)
        return c
    lax.fori_loop(0, 6, it, 0)
    o_ref[g] = u[g]

def newton(blocks, owner, G, owners=16):
    E = blocks.shape[0]
    sc = lambda *s: pltpu.VMEM(*s)
    return pl.pallas_call(
        functools.partial(newton_kernel, G, owners),
        grid_spec=pltpu.PrefetchScalarGridSpec(
            num_scalar_prefetch=1, grid=(E // G,),
            in_specs=[pl.BlockSpec((G, L, L), lambda i, f: (i, 0, 0))],
            out_specs=pl.BlockSpec((G, L, L), lambda i, f: (i, 0, 0)),
            scratch_shapes=[pltpu.VMEM((G, L, L), BF), pltpu.VMEM((G, L, L), F8), pltpu.VMEM((2, G, L, 2 * L), F8),
                pltpu.VMEM((G, L, L), F32), pltpu.VMEM((G, L, L), BF), pltpu.VMEM((G, L, L), F8),
                pltpu.VMEM((G, L, L), BF), pltpu.VMEM((G, L, L), F8), pltpu.VMEM((G, L, L), F8), pltpu.VMEM((G, L, L), F32)]),
        out_shape=jax.ShapeDtypeStruct(blocks.shape, F32),
        compiler_params=pltpu.CompilerParams(vmem_limit_bytes=60 * 2**20),
        name="newton")(owner, blocks)


def scale_kernel(elem_ref, p_ref, before_ref, after_ref, o_ref):
    t = pl.program_id(0)

    def multiply(b):
        p = p_ref[0]
        ph = p.astype(BF)
        plo = (p - ph.astype(F32)).astype(BF)
        bh = b.astype(BF)
        blo = (b - bh.astype(F32)).astype(BF)
        o_ref[0, 0] = mm(ph, blo) + mm(plo, bh) + mm(ph, bh)

    @pl.when(t < 2)
    def _():
        multiply(before_ref[0, 0])

    @pl.when(t >= 2)
    def _():
        multiply(after_ref[0, 0])


def scale(inverse, before, after, elem):
    return pl.pallas_call(
        scale_kernel,
        grid_spec=pltpu.PrefetchScalarGridSpec(
            num_scalar_prefetch=1, grid=(4,),
            in_specs=[
                pl.BlockSpec((1, L, L), lambda t, e: (e[t], 0, 0)),
                pl.BlockSpec((1, 1, L, L), lambda t, e: (0, jnp.minimum(t, 1), 0, 0)),
                pl.BlockSpec((1, 1, L, L), lambda t, e: (0, jnp.maximum(t - 2, 0), 0, 0)),
            ],
            out_specs=pl.BlockSpec((1, 1, L, L), lambda t, e: (t // 2, t % 2, 0, 0)),
        ),
        out_shape=jax.ShapeDtypeStruct((2, 2, L, L), F32),
        compiler_params=pltpu.CompilerParams(vmem_limit_bytes=56 * 2**20),
        name="scale",
    )(elem.reshape(-1), inverse, before, after)


def body(diag_blocks, outgoing, arrive_elem, owner_row):
    doms = lax.axis_size("dom")
    up = [(i, i + 1) for i in range(doms - 1)]
    down = [(j, i) for i, j in up]
    before = lax.ppermute(outgoing[1:2], "dom", up)
    after = lax.ppermute(outgoing[0:1], "dom", down)
    inverse = newton(diag_blocks, owner_row, 2, lax.axis_size("row"))
    return inverse, scale(inverse, before, after, arrive_elem)


def solution(mesh):
    return jax.shard_map(
        body,
        mesh=mesh,
        in_specs=(
            P(("dom", "row"), None, None),
            P("dom", "row", None, None),
            P("dom", "row"),
            P(("dom", "row")),
        ),
        out_specs=(P(("dom", "row"), None, None), P("dom", "row", None, None)),
        check_vma=False,
    )
```

```python
import functools
import jax
import jax.numpy as jnp
from jax import lax
from jax.experimental import pallas as pl
from jax.experimental.pallas import tpu as pltpu
from jax.sharding import PartitionSpec as P
F8 = jnp.float8_e4m3fn
BF = jnp.bfloat16
F32 = jnp.float32
L = 384
T = 128
C = 2.0**10
CLO = 2.0**8
TOL = 2.5e-4
TILES = [slice(i * T, (i + 1) * T) for i in range(L // T)]
M = 384

def mm(a, b):
    return jnp.dot(a, b, preferred_element_type=F32)

def newton_kernel(G, owners, flag_ref, a_ref, o_ref, rs, rb, rlo, w, acc, qb, q8, eb, e8, e2, col):
    step = pl.program_id(0)
    CH = [slice(i * M, (i + 1) * M) for i in range(L // M)]
    eye = lax.broadcasted_iota(jnp.int32, (T, T), 0) == lax.broadcasted_iota(jnp.int32, (T, T), 1)
    stiff = [flag_ref[step * G + g] < owners for g in range(G)]
    any_stiff = functools.reduce(jnp.logical_or, stiff)

    def point(g):
        o_ref[g] = jnp.zeros((L, L), F32)
        for t in TILES:
            d = jnp.sum(jnp.where(eye, a_ref[g, t, t], 0.0), axis=1, keepdims=True)
            o_ref[g, t, t] = jnp.where(eye, 1.0 / d, 0.0)

    @pl.when(jnp.logical_not(any_stiff))
    def _():
        for g in range(G):
            point(g)

    @pl.when(any_stiff)
    def _():
        for g in range(G):
            for t in TILES:
                d = jnp.where(eye, a_ref[g, t, t], 0.0)
                row = (-C) / jnp.sum(d, axis=0, keepdims=True)
                col[g, t] = jnp.broadcast_to((1.0 / C) / jnp.sum(d, axis=1, keepdims=True), (T, T))
                rs[g, :, t] = a_ref[g, :, t] * row
                rs[g, t, t] += jnp.where(eye, C, 0.0)
            r = rs[g]
            b = r.astype(BF)
            rb[g] = b
            rlo[g] = ((r - b.astype(F32)) * CLO).astype(F8)
            w[0, g, :, L:] = r.astype(F8)
        for g in range(G):
            for c in CH:
                s = mm(w[0, g, c, L:], w[0, g, :, L:]) * (1.0 / C)
                acc[g, c] = rs[g, c] + s
                w[0, g, c, :L] = s.astype(F8)
        for k in (1, 2):
            p, n = (k - 1) % 2, k % 2
            for g in range(G):
                for c in CH:
                    d = mm(w[p, g, c, :L], w[p, g]) * (1.0 / C)
                    s = d[:, :L]
                    q = acc[g, c] + d[:, L:]
                    w[n, g, c, :L] = s.astype(F8)
                    w[n, g, c, L:] = q.astype(F8)
                    acc[g, c] = q + s
        for g in range(G):
            for c in CH:
                q = acc[g, c] + mm(w[0, g, c, :L], w[0, g, :, L:]) * (1.0 / C)
                qb[g, c] = q.astype(BF)
                q8[g, c] = q.astype(F8)
        for g in range(G):
            for c in CH:
                e = (rs[g, c] - qb[g, c].astype(F32)) + (
                    mm(rb[g, c], qb[g]) * (1.0 / C) + mm(rlo[g, c], q8[g]) * (1.0 / (C * CLO)))
                acc[g, c] = e
                eb[g, c] = e.astype(BF)
                e8[g, c] = e.astype(F8)
        bad = []
        for g in range(G):
            ss = 0.0
            for c in CH:
                y = mm(e8[g, c], e8[g])
                q = qb[g, c].astype(F32) + (acc[g, c] + mm(qb[g, c], eb[g]) * (1.0 / C))
                q8[g, c] = q.astype(F8)
                e2[g, c] = y.astype(F8)
                acc[g, c] = q + y * (1.0 / C)
                ss = ss + jnp.sum(y * y, axis=0, keepdims=True)
            bad.append(jnp.logical_not(jnp.sum(ss) <= (TOL * C * C) ** 2 * L))
        for g in range(G):
            for i, c in enumerate(CH):
                x = acc[g, c] + mm(q8[g, c], e2[g]) * (1.0 / (C * C))
                for t in TILES:
                    z = x[:, t]
                    o_ref[g, c, t] = col[g, c] * z
            for t in TILES:
                o_ref[g, t, t] += jnp.where(eye, col[g, t] * C, 0.0)
        redo = [jnp.logical_or(jnp.logical_not(stiff[g]), bad[g]) for g in range(G)]

        @pl.when(functools.reduce(jnp.logical_or, redo))
        def _():
            for g in range(G):
                @pl.when(jnp.logical_not(stiff[g]))
                def _(g=g):
                    point(g)

                @pl.when(jnp.logical_and(stiff[g], bad[g]))
                def _(g=g):
                    slow(point, a_ref, o_ref, acc, g, eye)

def slow(point, a_ref, o_ref, acc, g, eye):
    HI = lax.Precision.HIGHEST
    point(g)
    def it(i, c):
        acc[g] = -jnp.dot(a_ref[g], o_ref[g], precision=HI, preferred_element_type=F32)
        for t in TILES:
            acc[g, t, t] += jnp.where(eye, 2.0, 0.0)
        o_ref[g] = jnp.dot(o_ref[g], acc[g], precision=HI, preferred_element_type=F32)
        return c
    lax.fori_loop(0, 6, it, 0)

def newton(blocks, owner, G, owners=16):
    E = blocks.shape[0]
    V = lambda t, *s: pltpu.VMEM((G, L) + (s or (L,)), t)
    return pl.pallas_call(
        functools.partial(newton_kernel, G, owners),
        grid_spec=pltpu.PrefetchScalarGridSpec(
            num_scalar_prefetch=1, grid=(E // G,),
            in_specs=[pl.BlockSpec((G, L, L), lambda i, f: (i, 0, 0))],
            out_specs=pl.BlockSpec((G, L, L), lambda i, f: (i, 0, 0)),
            scratch_shapes=[V(F32), V(BF), V(F8), pltpu.VMEM((2, G, L, 2 * L), F8),
                V(F32), V(BF), V(F8), V(BF), V(F8), V(F8), V(F32, T)]),
        out_shape=jax.ShapeDtypeStruct(blocks.shape, F32),
        compiler_params=pltpu.CompilerParams(vmem_limit_bytes=54 * 2**20),
        name="newton")(owner, blocks)


def scale_kernel(elem_ref, p_hbm, before_ref, after_ref, same_hbm, o_hbm, p, b, o, p_sem, b_sem, o_sem):
    def fetch(t):
        side = (before_ref, after_ref)[t // 2]
        return (
            pltpu.make_async_copy(p_hbm.at[elem_ref[t // 2, t % 2]], p.at[t], p_sem.at[t]),
            pltpu.make_async_copy(side.at[0, t % 2], b.at[t], b_sem.at[t]),
        )

    stores = [pltpu.make_async_copy(o.at[t], o_hbm.at[t // 2, t % 2], o_sem.at[t]) for t in range(4)]
    fetches = [fetch(t) for t in range(4)]
    for pair in fetches:
        for copy in pair:
            copy.start()
    for t in range(4):
        for copy in fetches[t]:
            copy.wait()
        ph = p[t].astype(BF)
        plo = (p[t] - ph.astype(F32)).astype(BF)
        bh = b[t].astype(BF)
        blo = (b[t] - bh.astype(F32)).astype(BF)
        o[t] = mm(ph, blo) + mm(plo, bh) + mm(ph, bh)
        stores[t].start()
    for store in stores:
        store.wait()


def scale(inverse, before, after, elem):
    hbm = pl.BlockSpec(memory_space=pltpu.HBM)
    anywhere = pl.BlockSpec(memory_space=pl.ANY)
    return pl.pallas_call(
        scale_kernel,
        in_specs=[pl.BlockSpec(memory_space=pltpu.SMEM), hbm, anywhere, anywhere],
        out_specs=[hbm, hbm],
        out_shape=[
            jax.ShapeDtypeStruct(inverse.shape, F32),
            jax.ShapeDtypeStruct((2, 2, L, L), F32),
        ],
        input_output_aliases={1: 0},
        scratch_shapes=[pltpu.VMEM((4, L, L), F32)] * 3 + [pltpu.SemaphoreType.DMA((4,))] * 3,
        compiler_params=pltpu.CompilerParams(vmem_limit_bytes=24 * 2**20),
        name="scale",
    )(elem, inverse, before, after)


def body(diag_blocks, outgoing, arrive_elem, owner_row):
    doms = lax.axis_size("dom")
    up = [(i, i + 1) for i in range(doms - 1)]
    down = [(j, i) for i, j in up]
    before = lax.ppermute(outgoing[1:2], "dom", up)
    after = lax.ppermute(outgoing[0:1], "dom", down)
    inverse = newton(diag_blocks, owner_row, 2, lax.axis_size("row"))
    return scale(inverse, before, after, arrive_elem)


def solution(mesh):
    return jax.shard_map(
        body,
        mesh=mesh,
        in_specs=(
            P(("dom", "row"), None, None),
            P("dom", "row", None, None),
            P("dom", "row"),
            P(("dom", "row")),
        ),
        out_specs=(P(("dom", "row"), None, None), P("dom", "row", None, None)),
        check_vma=False,
    )
```

```python
import functools
import jax
import jax.numpy as jnp
from jax import lax
from jax.experimental import pallas as pl
from jax.experimental.pallas import tpu as pltpu
from jax.sharding import PartitionSpec as P
F8 = jnp.float8_e4m3fn
BF = jnp.bfloat16
F32 = jnp.float32
L = 384
T = 128
C = 2.0**10
CLO = 2.0**8
TOL = 2.5e-4
TILES = [slice(i * T, (i + 1) * T) for i in range(L // T)]
M = 384

def mm(a, b):
    return jnp.dot(a, b, preferred_element_type=F32)

def newton_kernel(G, owners, flag_ref, a_ref, o_ref, rs, rb, rlo, ls, w, acc, qb, q8, p8, eb, e8, e2, col):
    step = pl.program_id(0)
    CH = [slice(i * M, (i + 1) * M) for i in range(L // M)]
    eye = lax.broadcasted_iota(jnp.int32, (T, T), 0) == lax.broadcasted_iota(jnp.int32, (T, T), 1)
    stiff = [flag_ref[step * G + g] < owners for g in range(G)]
    any_stiff = functools.reduce(jnp.logical_or, stiff)

    def point(g):
        o_ref[g] = jnp.zeros((L, L), F32)
        for t in TILES:
            d = jnp.sum(jnp.where(eye, a_ref[g, t, t], 0.0), axis=1, keepdims=True)
            o_ref[g, t, t] = jnp.where(eye, 1.0 / d, 0.0)

    @pl.when(jnp.logical_not(any_stiff))
    def _():
        for g in range(G):
            point(g)

    @pl.when(any_stiff)
    def _():
        for g in range(G):
            for t in TILES:
                d = jnp.where(eye, a_ref[g, t, t], 0.0)
                row = (-C) / jnp.sum(d, axis=0, keepdims=True)
                col[g, t] = jnp.broadcast_to((1.0 / C) / jnp.sum(d, axis=1, keepdims=True), (T, T))
                rs[g, :, t] = a_ref[g, :, t] * row
                rs[g, t, t] += jnp.where(eye, C, 0.0)
            r = rs[g]
            b = r.astype(BF)
            rb[g] = b
            rlo[g] = ((r - b.astype(F32)) * CLO).astype(F8)
            r = r.astype(F8)
            q8[g] = r
            for j, t in enumerate(TILES):
                w[0, g, :, 2 * j * T + T:2 * j * T + 2 * T] = r[:, t]
        for g in range(G):
            s = mm(q8[g], q8[g]) * (1.0 / C)
            acc[g] = rs[g] + s
            s = s.astype(F8)
            ls[0, g] = s
            for j, t in enumerate(TILES):
                w[0, g, :, 2 * j * T:2 * j * T + T] = s[:, t]
        for g in range(G):
            for j, t in enumerate(TILES):
                d = mm(ls[0, g], w[0, g, :, 2 * j * T:2 * j * T + 2 * T]) * (1.0 / C)
                s = d[:, :T]
                q = acc[g, :, t] + d[:, T:]
                acc[g, :, t] = q + s
                s = s.astype(F8)
                ls[1, g, :, t] = s
                w[1, g, :, 2 * j * T:2 * j * T + T] = s
                w[1, g, :, 2 * j * T + T:2 * j * T + 2 * T] = q.astype(F8)
        for g in range(G):
            for j, t in enumerate(TILES):
                d = mm(ls[1, g], w[1, g, :, 2 * j * T:2 * j * T + 2 * T]) * (1.0 / C)
                s = d[:, :T]
                q = acc[g, :, t] + d[:, T:]
                acc[g, :, t] = q + s
                ls[0, g, :, t] = s.astype(F8)
                q8[g, :, t] = q.astype(F8)
        for g in range(G):
            q = acc[g] + mm(ls[0, g], q8[g]) * (1.0 / C)
            qb[g] = q.astype(BF)
            p8[g] = q.astype(F8)
        for g in range(G):
            for c in CH:
                e = (rs[g, c] - qb[g, c].astype(F32)) + (
                    (mm(rb[g, c], qb[g]) + mm(rlo[g, c], p8[g]) * (1.0 / CLO)) * (1.0 / C))
                acc[g, c] = e
                eb[g, c] = e.astype(BF)
                e8[g, c] = e.astype(F8)
        bad = []
        for g in range(G):
            ss = 0.0
            for c in CH:
                y = mm(e8[g, c], e8[g])
                q = qb[g, c].astype(F32) + (acc[g, c] + mm(qb[g, c], eb[g]) * (1.0 / C))
                p8[g, c] = q.astype(F8)
                e2[g, c] = y.astype(F8)
                acc[g, c] = q + y * (1.0 / C)
                ss = ss + jnp.sum(y * y, axis=0, keepdims=True)
            bad.append(jnp.logical_not(jnp.sum(ss) <= (TOL * C * C) ** 2 * L))
        for g in range(G):
            for i, c in enumerate(CH):
                x = acc[g, c] + mm(p8[g, c], e2[g]) * (1.0 / (C * C))
                for t in TILES:
                    z = x[:, t]
                    o_ref[g, c, t] = col[g, c] * z
            for t in TILES:
                o_ref[g, t, t] += jnp.where(eye, col[g, t] * C, 0.0)
        redo = [jnp.logical_or(jnp.logical_not(stiff[g]), bad[g]) for g in range(G)]

        @pl.when(functools.reduce(jnp.logical_or, redo))
        def _():
            for g in range(G):
                @pl.when(jnp.logical_not(stiff[g]))
                def _(g=g):
                    point(g)

                @pl.when(jnp.logical_and(stiff[g], bad[g]))
                def _(g=g):
                    slow(point, a_ref, o_ref, acc, g, eye)

def slow(point, a_ref, o_ref, acc, g, eye):
    HI = lax.Precision.HIGHEST
    point(g)
    def it(i, c):
        acc[g] = -jnp.dot(a_ref[g], o_ref[g], precision=HI, preferred_element_type=F32)
        for t in TILES:
            acc[g, t, t] += jnp.where(eye, 2.0, 0.0)
        o_ref[g] = jnp.dot(o_ref[g], acc[g], precision=HI, preferred_element_type=F32)
        return c
    lax.fori_loop(0, 6, it, 0)

def newton(blocks, owner, G, owners=16):
    E = blocks.shape[0]
    V = lambda t, *s: pltpu.VMEM((G, L) + (s or (L,)), t)
    return pl.pallas_call(
        functools.partial(newton_kernel, G, owners),
        grid_spec=pltpu.PrefetchScalarGridSpec(
            num_scalar_prefetch=1, grid=(E // G,),
            in_specs=[pl.BlockSpec((G, L, L), lambda i, f: (i, 0, 0))],
            out_specs=pl.BlockSpec((G, L, L), lambda i, f: (i, 0, 0)),
            scratch_shapes=[V(F32), V(BF), V(F8), pltpu.VMEM((2, G, L, L), F8), pltpu.VMEM((2, G, L, 2 * L), F8),
                V(F32), V(BF), V(F8), V(F8), V(BF), V(F8), V(F8), V(F32, T)]),
        out_shape=jax.ShapeDtypeStruct(blocks.shape, F32),
        compiler_params=pltpu.CompilerParams(vmem_limit_bytes=54 * 2**20),
        name="newton")(owner, blocks)


def scale_kernel(elem_ref, p_hbm, before_ref, after_ref, same_hbm, o_hbm, p, b, o, p_sem, o_sem):
    fetches = [pltpu.make_async_copy(p_hbm.at[elem_ref[t // 2, t % 2]], p.at[t], p_sem.at[t]) for t in range(4)]
    stores = [pltpu.make_async_copy(o.at[t], o_hbm.at[t // 2, t % 2], o_sem.at[t]) for t in range(4)]
    for copy in fetches:
        copy.start()
    for t in range(4):
        x = (before_ref, after_ref)[t // 2][0, t % 2]
        hi = x.astype(BF)
        b[t, :, :L] = hi
        b[t, :, L:] = (x - hi.astype(F32)).astype(BF)
    for pair in ((0, 1), (2, 3)):
        for t in pair:
            fetches[t].wait()
        for t in pair:
            hi = p[t].astype(BF)
            lo = (p[t] - hi.astype(F32)).astype(BF)
            d = mm(hi, b[t])
            o[t] = d[:, :L] + (d[:, L:] + mm(lo, b[t, :, :L]))
        for t in pair:
            stores[t].start()
    for store in stores:
        store.wait()


def scale(inverse, before, after, elem):
    hbm = pl.BlockSpec(memory_space=pltpu.HBM)
    vmem = pl.BlockSpec(memory_space=pltpu.VMEM)
    return pl.pallas_call(
        scale_kernel,
        in_specs=[pl.BlockSpec(memory_space=pltpu.SMEM), hbm, vmem, vmem],
        out_specs=[hbm, hbm],
        out_shape=[jax.ShapeDtypeStruct(inverse.shape, F32), jax.ShapeDtypeStruct((2, 2, L, L), F32)],
        input_output_aliases={1: 0},
        scratch_shapes=[pltpu.VMEM((4, L, L), F32), pltpu.VMEM((4, L, 2 * L), BF), pltpu.VMEM((4, L, L), F32),
            pltpu.SemaphoreType.DMA((4,)), pltpu.SemaphoreType.DMA((4,))],
        compiler_params=pltpu.CompilerParams(vmem_limit_bytes=24 * 2**20),
        name="scale",
    )(elem, inverse, before, after)


def body(diag_blocks, outgoing, arrive_elem, owner_row):
    doms = lax.axis_size("dom")
    up = [(i, i + 1) for i in range(doms - 1)]
    down = [(j, i) for i, j in up]
    before = lax.ppermute(outgoing[1:2], "dom", up)
    after = lax.ppermute(outgoing[0:1], "dom", down)
    inverse = newton(diag_blocks, owner_row, 2, lax.axis_size("row"))
    return scale(inverse, before, after, arrive_elem)


def solution(mesh):
    return jax.shard_map(
        body,
        mesh=mesh,
        in_specs=(
            P(("dom", "row"), None, None),
            P("dom", "row", None, None),
            P("dom", "row"),
            P(("dom", "row")),
        ),
        out_specs=(P(("dom", "row"), None, None), P("dom", "row", None, None)),
        check_vma=False,
    )
```

```python
import functools
import jax
import jax.numpy as jnp
from jax import lax
from jax.experimental import pallas as pl
from jax.experimental.pallas import tpu as pltpu
from jax.sharding import PartitionSpec as P
F8 = jnp.float8_e4m3fn
BF = jnp.bfloat16
F32 = jnp.float32
L = 384
T = 128
C = 2.0**10
CLO = 2.0**8
TOL = 2.5e-4
WIDE = [slice(0, 256), slice(256, 384)]
TILES = [slice(i * T, (i + 1) * T) for i in range(L // T)]
M = 384

def mm(a, b):
    return jnp.dot(a, b, preferred_element_type=F32)

def newton_kernel(G, owners, flag_ref, a_ref, o_ref, rs, rb, rlo, ls, w, acc, qb, q8, p8, eb, e8, e2, col):
    step = pl.program_id(0)
    CH = [slice(i * M, (i + 1) * M) for i in range(L // M)]
    eye = lax.broadcasted_iota(jnp.int32, (T, T), 0) == lax.broadcasted_iota(jnp.int32, (T, T), 1)
    stiff = [flag_ref[step * G + g] < owners for g in range(G)]
    any_stiff = functools.reduce(jnp.logical_or, stiff)

    def point(g):
        o_ref[g] = jnp.zeros((L, L), F32)
        for t in TILES:
            d = jnp.sum(jnp.where(eye, a_ref[g, t, t], 0.0), axis=1, keepdims=True)
            o_ref[g, t, t] = jnp.where(eye, 1.0 / d, 0.0)

    @pl.when(jnp.logical_not(any_stiff))
    def _():
        for g in range(G):
            point(g)

    @pl.when(any_stiff)
    def _():
        for g in range(G):
            for t in TILES:
                d = jnp.where(eye, a_ref[g, t, t], 0.0)
                row = (-C) / jnp.sum(d, axis=0, keepdims=True)
                col[g, t] = jnp.broadcast_to((1.0 / C) / jnp.sum(d, axis=1, keepdims=True), (T, T))
                rs[g, :, t] = a_ref[g, :, t] * row
                rs[g, t, t] += jnp.where(eye, C, 0.0)
            r = rs[g]
            b = r.astype(BF)
            rb[g] = b
            rlo[g] = ((r - b.astype(F32)) * CLO).astype(F8)
            r = r.astype(F8)
            q8[g] = r
            for j, t in enumerate(TILES):
                w[0, g, :, 2 * j * T + T:2 * j * T + 2 * T] = r[:, t]
        for g in range(G):
            s = mm(q8[g], q8[g]) * (1.0 / C)
            acc[g] = rs[g] + s
            s = s.astype(F8)
            ls[0, g] = s
            for j, t in enumerate(TILES):
                w[0, g, :, 2 * j * T:2 * j * T + T] = s[:, t]
        for g in range(G):
            for j, t in enumerate(TILES):
                d = mm(ls[0, g], w[0, g, :, 2 * j * T:2 * j * T + 2 * T]) * (1.0 / C)
                s = d[:, :T]
                q = acc[g, :, t] + d[:, T:]
                acc[g, :, t] = q + s
                s = s.astype(F8)
                ls[1, g, :, t] = s
                w[1, g, :, 2 * j * T:2 * j * T + T] = s
                w[1, g, :, 2 * j * T + T:2 * j * T + 2 * T] = q.astype(F8)
        for g in range(G):
            for j, t in enumerate(TILES):
                d = mm(ls[1, g], w[1, g, :, 2 * j * T:2 * j * T + 2 * T]) * (1.0 / C)
                s = d[:, :T]
                q = acc[g, :, t] + d[:, T:]
                acc[g, :, t] = q + s
                ls[0, g, :, t] = s.astype(F8)
                q8[g, :, t] = q.astype(F8)
        for g in range(G):
            q = acc[g] + mm(ls[0, g], q8[g]) * (1.0 / C)
            qb[g] = q.astype(BF)
            p8[g] = q.astype(F8)
        for g in range(G):
            for c in WIDE:
                u = mm(rb[g], qb[g, :, c]) + mm(rlo[g], p8[g, :, c]) * (1.0 / CLO)
                e = (rs[g, :, c] - qb[g, :, c].astype(F32)) + u * (1.0 / C)
                acc[g, :, c] = e
                eb[g, :, c] = e.astype(BF)
                e8[g, :, c] = e.astype(F8)
        bad = []
        for g in range(G):
            ss = 0.0
            for c in WIDE:
                y = mm(e8[g], e8[g, :, c])
                q = qb[g, :, c].astype(F32) + (acc[g, :, c] + mm(qb[g], eb[g, :, c]) * (1.0 / C))
                p8[g, :, c] = q.astype(F8)
                e2[g, :, c] = y.astype(F8)
                acc[g, :, c] = q + y * (1.0 / C)
                z = y[:, :T] * y[:, :T]
                ss = ss + (z if c.stop == L else z + y[:, T:] * y[:, T:])
            bad.append(jnp.logical_not(jnp.sum(ss) <= (TOL * C * C) ** 2 * L))
        for g in range(G):
            for i, c in enumerate(CH):
                x = acc[g, c] + mm(p8[g, c], e2[g]) * (1.0 / (C * C))
                for t in TILES:
                    z = x[:, t]
                    o_ref[g, c, t] = col[g, c] * z
            for t in TILES:
                o_ref[g, t, t] += jnp.where(eye, col[g, t] * C, 0.0)
        redo = [jnp.logical_or(jnp.logical_not(stiff[g]), bad[g]) for g in range(G)]

        @pl.when(functools.reduce(jnp.logical_or, redo))
        def _():
            for g in range(G):
                @pl.when(jnp.logical_not(stiff[g]))
                def _(g=g):
                    point(g)

                @pl.when(jnp.logical_and(stiff[g], bad[g]))
                def _(g=g):
                    slow(point, a_ref, o_ref, acc, g, eye)

def slow(point, a_ref, o_ref, acc, g, eye):
    HI = lax.Precision.HIGHEST
    point(g)
    def it(i, c):
        acc[g] = -jnp.dot(a_ref[g], o_ref[g], precision=HI, preferred_element_type=F32)
        for t in TILES:
            acc[g, t, t] += jnp.where(eye, 2.0, 0.0)
        o_ref[g] = jnp.dot(o_ref[g], acc[g], precision=HI, preferred_element_type=F32)
        return c
    lax.fori_loop(0, 6, it, 0)

def newton(blocks, owner, G, owners=16):
    E = blocks.shape[0]
    V = lambda t, *s: pltpu.VMEM((G, L) + (s or (L,)), t)
    return pl.pallas_call(
        functools.partial(newton_kernel, G, owners),
        grid_spec=pltpu.PrefetchScalarGridSpec(
            num_scalar_prefetch=1, grid=(E // G,),
            in_specs=[pl.BlockSpec((G, L, L), lambda i, f: (i, 0, 0))],
            out_specs=pl.BlockSpec((G, L, L), lambda i, f: (i, 0, 0)),
            scratch_shapes=[V(F32), V(BF), V(F8), pltpu.VMEM((2, G, L, L), F8), pltpu.VMEM((2, G, L, 2 * L), F8),
                V(F32), V(BF), V(F8), V(F8), V(BF), V(F8), V(F8), V(F32, T)]),
        out_shape=jax.ShapeDtypeStruct(blocks.shape, F32),
        compiler_params=pltpu.CompilerParams(vmem_limit_bytes=54 * 2**20),
        name="newton")(owner, blocks)


def scale_kernel(elem_ref, p_hbm, before_ref, after_ref, same_hbm, o_hbm, p, b, o, p_sem, o_sem):
    fetches = [pltpu.make_async_copy(p_hbm.at[elem_ref[t // 2, t % 2]], p.at[t], p_sem.at[t]) for t in range(4)]
    stores = [pltpu.make_async_copy(o.at[t], o_hbm.at[t // 2, t % 2], o_sem.at[t]) for t in range(4)]
    for copy in fetches:
        copy.start()
    for t in range(4):
        x = (before_ref, after_ref)[t // 2][0, t % 2]
        hi = x.astype(BF)
        b[t, :, :L] = hi
        b[t, :, L:] = (x - hi.astype(F32)).astype(BF)
    for pair in ((0, 1), (2, 3)):
        for t in pair:
            fetches[t].wait()
        for t in pair:
            hi = p[t].astype(BF)
            lo = (p[t] - hi.astype(F32)).astype(BF)
            d = mm(hi, b[t])
            o[t] = d[:, :L] + (d[:, L:] + mm(lo, b[t, :, :L]))
        for t in pair:
            stores[t].start()
    for store in stores:
        store.wait()


def scale(inverse, before, after, elem):
    hbm = pl.BlockSpec(memory_space=pltpu.HBM)
    vmem = pl.BlockSpec(memory_space=pltpu.VMEM)
    return pl.pallas_call(
        scale_kernel,
        in_specs=[pl.BlockSpec(memory_space=pltpu.SMEM), hbm, vmem, vmem],
        out_specs=[hbm, hbm],
        out_shape=[jax.ShapeDtypeStruct(inverse.shape, F32), jax.ShapeDtypeStruct((2, 2, L, L), F32)],
        input_output_aliases={1: 0},
        scratch_shapes=[pltpu.VMEM((4, L, L), F32), pltpu.VMEM((4, L, 2 * L), BF), pltpu.VMEM((4, L, L), F32),
            pltpu.SemaphoreType.DMA((4,)), pltpu.SemaphoreType.DMA((4,))],
        compiler_params=pltpu.CompilerParams(vmem_limit_bytes=24 * 2**20),
        name="scale",
    )(elem, inverse, before, after)


def body(diag_blocks, outgoing, arrive_elem, owner_row):
    doms = lax.axis_size("dom")
    up = [(i, i + 1) for i in range(doms - 1)]
    down = [(j, i) for i, j in up]
    before = lax.ppermute(outgoing[1:2], "dom", up)
    after = lax.ppermute(outgoing[0:1], "dom", down)
    inverse = newton(diag_blocks, owner_row, 2, lax.axis_size("row"))
    return scale(inverse, before, after, arrive_elem)


def solution(mesh):
    return jax.shard_map(
        body,
        mesh=mesh,
        in_specs=(
            P(("dom", "row"), None, None),
            P("dom", "row", None, None),
            P("dom", "row"),
            P(("dom", "row")),
        ),
        out_specs=(P(("dom", "row"), None, None), P("dom", "row", None, None)),
        check_vma=False,
    )
```

```python
import functools
import jax
import jax.numpy as jnp
from jax import lax
from jax.experimental import pallas as pl
from jax.experimental.pallas import tpu as pltpu
from jax.sharding import PartitionSpec as P
F8 = jnp.float8_e4m3fn
BF = jnp.bfloat16
F32 = jnp.float32
L = 384
T = 128
C = 2.0**10
CLO = 2.0**8
TOL = 2.5e-4
WIDE = [slice(0, 256), slice(256, 384)]
TILES = [slice(i * T, (i + 1) * T) for i in range(L // T)]
M = 384

def mm(a, b):
    return jnp.dot(a, b, preferred_element_type=F32)

def newton_kernel(G, owners, flag_ref, a_ref, o_ref, rs, rb, rlo, ls, w, acc, qb, q8, p8, eb, e8, e2, col):
    step = pl.program_id(0)
    CH = [slice(i * M, (i + 1) * M) for i in range(L // M)]
    eye = lax.broadcasted_iota(jnp.int32, (T, T), 0) == lax.broadcasted_iota(jnp.int32, (T, T), 1)
    stiff = [flag_ref[step * G + g] < owners for g in range(G)]
    any_stiff = functools.reduce(jnp.logical_or, stiff)

    def point(g):
        o_ref[g] = jnp.zeros((L, L), F32)
        for t in TILES:
            d = jnp.sum(jnp.where(eye, a_ref[g, t, t], 0.0), axis=1, keepdims=True)
            o_ref[g, t, t] = jnp.where(eye, 1.0 / d, 0.0)

    @pl.when(jnp.logical_not(any_stiff))
    def _():
        for g in range(G):
            point(g)

    @pl.when(any_stiff)
    def _():
        for g in range(G):
            for t in TILES:
                d = jnp.where(eye, a_ref[g, t, t], 0.0)
                row = (-C) / jnp.sum(d, axis=0, keepdims=True)
                col[g, t] = jnp.broadcast_to((1.0 / C) / jnp.sum(d, axis=1, keepdims=True), (T, T))
                rs[g, :, t] = a_ref[g, :, t] * row
                rs[g, t, t] += jnp.where(eye, C, 0.0)
            r = rs[g]
            b = r.astype(BF)
            rb[g] = b
            rlo[g] = ((r - b.astype(F32)) * CLO).astype(F8)
            r = r.astype(F8)
            q8[g] = r
            for j, t in enumerate(TILES):
                w[0, g, :, 2 * j * T + T:2 * j * T + 2 * T] = r[:, t]
        for g in range(G):
            s = mm(q8[g], q8[g]) * (1.0 / C)
            acc[g] = rs[g] + s
            s = s.astype(F8)
            ls[0, g] = s
            for j, t in enumerate(TILES):
                w[0, g, :, 2 * j * T:2 * j * T + T] = s[:, t]
        for g in range(G):
            for j, t in enumerate(TILES):
                d = mm(ls[0, g], w[0, g, :, 2 * j * T:2 * j * T + 2 * T]) * (1.0 / C)
                s = d[:, :T]
                q = acc[g, :, t] + d[:, T:]
                acc[g, :, t] = q + s
                s = s.astype(F8)
                ls[1, g, :, t] = s
                w[1, g, :, 2 * j * T:2 * j * T + T] = s
                w[1, g, :, 2 * j * T + T:2 * j * T + 2 * T] = q.astype(F8)
        for g in range(G):
            for j, t in enumerate(TILES):
                d = mm(ls[1, g], w[1, g, :, 2 * j * T:2 * j * T + 2 * T]) * (1.0 / C)
                s = d[:, :T]
                q = acc[g, :, t] + d[:, T:]
                acc[g, :, t] = q + s
                ls[0, g, :, t] = s.astype(F8)
                q8[g, :, t] = q.astype(F8)
        for g in range(G):
            q = acc[g] + mm(ls[0, g], q8[g]) * (1.0 / C)
            qb[g] = q.astype(BF)
            p8[g] = q.astype(F8)
        for g in range(G):
            for c in WIDE:
                u = mm(rb[g], qb[g, :, c]) + mm(rlo[g], p8[g, :, c]) * (1.0 / CLO)
                e = (rs[g, :, c] - qb[g, :, c].astype(F32)) + u * (1.0 / C)
                acc[g, :, c] = e
                eb[g, :, c] = e.astype(BF)
                e8[g, :, c] = e.astype(F8)
        bad = []
        for g in range(G):
            ss = 0.0
            for c in WIDE:
                y = mm(e8[g], e8[g, :, c])
                q = qb[g, :, c].astype(F32) + (acc[g, :, c] + mm(qb[g], eb[g, :, c]) * (1.0 / C))
                p8[g, :, c] = q.astype(F8)
                e2[g, :, c] = y.astype(F8)
                acc[g, :, c] = q + y * (1.0 / C)
                z = y[:, :T] * y[:, :T]
                ss = ss + (z if c.stop == L else z + y[:, T:] * y[:, T:])
            bad.append(jnp.logical_not(jnp.sum(ss) <= (TOL * C * C) ** 2 * L))
        for g in range(G):
            for i, c in enumerate(CH):
                x = acc[g, c] + mm(p8[g, c], e2[g]) * (1.0 / (C * C))
                for t in TILES:
                    z = x[:, t]
                    o_ref[g, c, t] = col[g, c] * z
            for t in TILES:
                o_ref[g, t, t] += jnp.where(eye, col[g, t] * C, 0.0)
        redo = [jnp.logical_or(jnp.logical_not(stiff[g]), bad[g]) for g in range(G)]

        @pl.when(functools.reduce(jnp.logical_or, redo))
        def _():
            for g in range(G):
                @pl.when(jnp.logical_not(stiff[g]))
                def _(g=g):
                    point(g)

                @pl.when(jnp.logical_and(stiff[g], bad[g]))
                def _(g=g):
                    slow(point, a_ref, o_ref, acc, g, eye)

def slow(point, a_ref, o_ref, acc, g, eye):
    HI = lax.Precision.HIGHEST
    point(g)
    def it(i, c):
        acc[g] = -jnp.dot(a_ref[g], o_ref[g], precision=HI, preferred_element_type=F32)
        for t in TILES:
            acc[g, t, t] += jnp.where(eye, 2.0, 0.0)
        o_ref[g] = jnp.dot(o_ref[g], acc[g], precision=HI, preferred_element_type=F32)
        return c
    lax.fori_loop(0, 6, it, 0)

def newton(blocks, owner, G, owners=16):
    E = blocks.shape[0]
    V = lambda t, *s: pltpu.VMEM((G, L) + (s or (L,)), t)
    return pl.pallas_call(
        functools.partial(newton_kernel, G, owners),
        grid_spec=pltpu.PrefetchScalarGridSpec(
            num_scalar_prefetch=1, grid=(E // G,),
            in_specs=[pl.BlockSpec((G, L, L), lambda i, f: (i, 0, 0))],
            out_specs=pl.BlockSpec((G, L, L), lambda i, f: (i, 0, 0)),
            scratch_shapes=[V(F32), V(BF), V(F8), pltpu.VMEM((2, G, L, L), F8), pltpu.VMEM((2, G, L, 2 * L), F8),
                V(F32), V(BF), V(F8), V(F8), V(BF), V(F8), V(F8), V(F32, T)]),
        out_shape=jax.ShapeDtypeStruct(blocks.shape, F32),
        compiler_params=pltpu.CompilerParams(vmem_limit_bytes=54 * 2**20),
        name="newton")(owner, blocks)


def scale_kernel(elem_ref, p_hbm, near_ref, far_ref, same_hbm, o_hbm, p, b, o, p_sem, o_sem):
    odd = lax.rem(lax.axis_index("dom"), 2)
    sides = [1 - odd, 1 - odd, odd, odd]
    fetches = [pltpu.make_async_copy(p_hbm.at[elem_ref[sides[t], t % 2]], p.at[t], p_sem.at[t]) for t in range(4)]
    stores = [pltpu.make_async_copy(o.at[t], o_hbm.at[sides[t], t % 2], o_sem.at[t]) for t in range(4)]
    for copy in fetches:
        copy.start()
    for t in range(4):
        x = near_ref[odd, t % 2] if t < 2 else far_ref[0, t % 2]
        hi = x.astype(BF)
        b[t, :, :L] = hi
        b[t, :, L:] = (x - hi.astype(F32)).astype(BF)
    for pair in ((0, 1), (2, 3)):
        for t in pair:
            fetches[t].wait()
        for t in pair:
            hi = p[t].astype(BF)
            lo = (p[t] - hi.astype(F32)).astype(BF)
            d = mm(hi, b[t])
            o[t] = d[:, :L] + (d[:, L:] + mm(lo, b[t, :, :L]))
        for t in pair:
            stores[t].start()
    for store in stores:
        store.wait()


def scale(inverse, near, far, elem):
    hbm = pl.BlockSpec(memory_space=pltpu.HBM)
    vmem = pl.BlockSpec(memory_space=pltpu.VMEM)
    return pl.pallas_call(
        scale_kernel,
        in_specs=[pl.BlockSpec(memory_space=pltpu.SMEM), hbm, vmem, vmem],
        out_specs=[hbm, hbm],
        out_shape=[jax.ShapeDtypeStruct(inverse.shape, F32), jax.ShapeDtypeStruct((2, 2, L, L), F32)],
        input_output_aliases={1: 0},
        scratch_shapes=[pltpu.VMEM((4, L, L), F32), pltpu.VMEM((4, L, 2 * L), BF), pltpu.VMEM((4, L, L), F32),
            pltpu.SemaphoreType.DMA((4,)), pltpu.SemaphoreType.DMA((4,))],
        compiler_params=pltpu.CompilerParams(vmem_limit_bytes=24 * 2**20),
        name="scale",
    )(elem, inverse, near, far)


def body(diag_blocks, outgoing, arrive_elem, owner_row):
    doms = lax.axis_size("dom")
    odd = lax.axis_index("dom") % 2
    chip = [(i, i ^ 1) for i in range(doms)]
    between = [(i, j) for k in range(1, doms - 1, 2) for i, j in ((k, k + 1), (k + 1, k))]
    near = lax.ppermute(outgoing, "dom", chip)
    far = lax.ppermute(lax.dynamic_slice_in_dim(outgoing, odd, 1, axis=0), "dom", between)
    inverse = newton(diag_blocks, owner_row, 2, lax.axis_size("row"))
    return scale(inverse, near, far, arrive_elem)


def solution(mesh):
    return jax.shard_map(
        body,
        mesh=mesh,
        in_specs=(
            P(("dom", "row"), None, None),
            P("dom", "row", None, None),
            P("dom", "row"),
            P(("dom", "row")),
        ),
        out_specs=(P(("dom", "row"), None, None), P("dom", "row", None, None)),
        check_vma=False,
    )
```
